256 devices in a mesh: inst: 16 (over x_lo, z), mesh: 16 (over x_hi, y, core).
Axes of the slice: x: 4 (x_hi: 2, x_lo: 2; x = x_hi * 2 + x_lo), y: 4, z: 8, core: 2. Of those that a mesh axis runs over, the one named last changes fastest.
Arguments:
- tangent_in: bfloat16 [16, 4, 64, 2048], P('inst', None, None, 'mesh'), may hold values from -6 to 6
- adjoint_in: bfloat16 [16, 4, 64, 2048], P('inst', None, None, 'mesh'), may hold values from -6 to 6
- jacobian: bfloat16 [16, 5, 64, 64, 2048], P('inst', None, None, None, 'mesh'), may hold values from -0.3125 to 0.3125
- neighbors: int32 [2, 4, 2048], P(None, None, 'mesh'), may hold values from 0 to 192, as said below
- send_low: int32 [2, 512], P(None, 'mesh'), may hold values from 0 to 127, as said below
- send_high: int32 [2, 512], P(None, 'mesh'), may hold values from 0 to 127, as said below
- frequency: float32 [1], replicated, may hold values from 0.05 to 0.2
Outputs:
- tangent_out: bfloat16 [16, 4, 64, 2048], P('inst', None, None, 'mesh')
- adjoint_out: bfloat16 [16, 4, 64, 2048], P('inst', None, None, 'mesh')
The draws below stay inside these ranges and needn't reach their ends.
Inputs may be any that keep to these rules, and one draw needn't show every extreme that they name: `neighbors`: extended row indices: below 128 a row of the slab itself, 128 to 159 rows received from the slab below, the next 32 rows received from the slab above, 192 the zero row. `send_low`: each slab's 32 entries are distinct block rows of that slab. `send_high`: each slab's 32 entries are distinct block rows of that slab.
All inputs are finite; a program needn't handle non-finite values.
Results may differ from the reference program's by a relative error of at most 0.003.
Values may be sent and summed in bfloat16 or wider, within the bound.
No kernel may reach another device: no remote copies, remote signals or barrier semaphores. Data moves between devices by JAX's collectives and lax.ppermute only.
A program may use at most 64 MiB of HBM per device.

```python
import math
import jax
import jax.numpy as jnp
from jax import lax

BLK = 64
COLS = 4
NNB = 4
INST = 8
NB = 128
HALO = 32
SIDES = 2
MROWS = 2048
ROWS = 4096


def draw_neighbors(key, part):
    slabs = ROWS // NB
    index = jax.random.randint(jax.random.fold_in(key, 5), (NNB, slabs, NB), 0, NB + 2 * HALO + 1)
    where_pad = jax.random.randint(jax.random.fold_in(key, 6), (slabs,), 0, NB)
    where_zero = jax.random.randint(jax.random.fold_in(key, 7), (slabs,), 0, NB)
    slab_ids = jnp.arange(slabs)
    index = index.at[0, slab_ids, where_pad].set(NB + 2 * HALO)
    index = index.at[1, slab_ids, where_zero].set(0)
    return index.reshape(NNB, SIDES, MROWS).transpose(1, 0, 2).astype(jnp.int32)


def pick_rows(key):
    slabs = ROWS // NB
    keys = jax.random.split(jax.random.fold_in(key, 1), slabs)
    inner = jax.vmap(lambda one_key: jax.random.permutation(one_key, NB - 2))(keys)[:, :HALO - 2] + 1
    ends = jnp.broadcast_to(jnp.array([0, NB - 1], dtype=jnp.int32), (slabs, 2))
    joined = jnp.concatenate([inner.astype(jnp.int32), ends], axis=1)
    order_keys = jax.random.split(jax.random.fold_in(key, 2), slabs)
    order = jax.vmap(lambda one_key: jax.random.permutation(one_key, HALO))(order_keys)
    rows = jnp.take_along_axis(joined, order, axis=1)
    return rows.reshape(SIDES, MROWS // 4).astype(jnp.int32)


def draw_send_low(key, part):
    return pick_rows(jax.random.fold_in(key, 11))


def draw_send_high(key, part):
    return pick_rows(jax.random.fold_in(key, 23))


def block_levels(own_key, dims, shards, smallest, top_value):
    level, own = 1.0, jax.random.fold_in(own_key, 6)
    for axis_at, shards_of in shards:
        steps = jnp.exp(jax.random.uniform(jax.random.fold_in(own, axis_at), (shards_of,), jnp.float32, smallest / len(shards), top_value / len(shards)))
        level = level * jnp.repeat(steps, dims[axis_at] // shards_of).reshape([-1 if axis == axis_at else 1 for axis in range(len(dims))])
    return level


def noise(key, extent, scale, bound, cuts=(), kind=jnp.bfloat16):
    drawn = jax.random.normal(key, extent, jnp.float32) * scale
    if len(cuts) > 0:
        drawn = block_levels(key, extent, cuts, -0.22, 0.18) * drawn
    return jnp.clip(drawn, min=-bound, max=bound).astype(kind)


def setup_inputs(seed: int = 0) -> dict:
    key_of = jax.random.split(jax.random.key(seed), 8)
    return {
        "tangent_in": noise(key_of[0], (INST * SIDES, COLS, BLK, MROWS), 1.0, 6.0, ((0, 16), (3, 16))),
        "adjoint_in": noise(key_of[1], (INST * SIDES, COLS, BLK, MROWS), 1.0, 6.0, ((0, 16), (3, 16))),
        "jacobian": noise(key_of[2], (INST * SIDES, NNB + 1, BLK, BLK, MROWS), (BLK * (NNB + 1)) ** -0.5, 0.3125, ((0, 16), (4, 16))),
        "neighbors": draw_neighbors(jax.random.fold_in(key_of[7], 71), 0),
        "send_low": draw_send_low(jax.random.fold_in(key_of[7], 71), 0),
        "send_high": draw_send_high(jax.random.fold_in(key_of[7], 71), 0),
        "frequency": jnp.clip(jnp.exp(jax.random.uniform(key_of[6], (1,), jnp.float32, math.log(0.05), math.log(0.2))), 0.05, 0.2),
    }


def spectral_table(row_ids, col_ids, count, frequency):
    offset = row_ids[:, None] - col_ids[None, :]
    phase = offset.astype(jnp.float32) * (math.pi / count)
    parity = 1.0 - 2.0 * jnp.remainder(offset, 2).astype(jnp.float32)
    denom = jnp.where(offset == 0, 1.0, jnp.sin(phase))
    value = jnp.where(offset == 0, 0.0, parity * jnp.cos(phase) / denom)
    return value * (0.5 * frequency[0])


def take_slab(values, index):
    return jax.vmap(lambda part_v, part_i: jnp.take(part_v, part_i, axis=1), in_axes=(1, 0), out_axes=1)(values, index)


def add_slab(target, index, values):
    return jax.vmap(lambda part_t, part_i, part_v: part_t.at[:, part_i].add(part_v), in_axes=(1, 0, 1), out_axes=1)(target, index, values)


def to_rows(panel):
    return panel.reshape(INST, SIDES, COLS, BLK, MROWS).transpose(0, 2, 3, 1, 4).reshape(INST, COLS, BLK, ROWS)


def from_rows(panel):
    return panel.reshape(INST, COLS, BLK, SIDES, MROWS).transpose(0, 3, 1, 2, 4).reshape(INST * SIDES, COLS, BLK, MROWS)


def reference(tangent_in, adjoint_in, jacobian, neighbors, send_low, send_high, frequency):
    tangent_rows = to_rows(tangent_in)
    adjoint_rows = to_rows(adjoint_in)
    inst_count = INST
    slabs = ROWS // NB
    lead = inst_count * COLS * BLK
    width = NB + 2 * HALO + 1
    flat_x = tangent_rows.reshape(lead, slabs, NB)
    low_idx = send_low.reshape(slabs, HALO)
    high_idx = send_high.reshape(slabs, HALO)
    nbr = neighbors.transpose(1, 0, 2).reshape(NNB, slabs, NB)
    rows_high = take_slab(flat_x, high_idx)
    rows_low = take_slab(flat_x, low_idx)
    edge = jnp.zeros((lead, 1, HALO), tangent_in.dtype)
    below = jnp.concatenate([edge, rows_high[:, :-1]], axis=1)
    above = jnp.concatenate([rows_low[:, 1:], edge], axis=1)
    blank = jnp.zeros((lead, slabs, 1), tangent_in.dtype)
    extended = jnp.concatenate([flat_x, below, above, blank], axis=2).reshape(inst_count, COLS, BLK, slabs, width)
    adjoint_view = adjoint_rows.reshape(inst_count, COLS, BLK, slabs, NB)
    jac_all = jacobian.reshape(INST, SIDES, NNB + 1, BLK, BLK, MROWS)

    def one_instance(inputs):
        jac, ext, weights = inputs
        jac = jac.transpose(1, 2, 3, 0, 4).reshape(NNB + 1, BLK, BLK, slabs, NB).astype(jnp.float32)
        picked = [ext[..., :NB]]
        for slot in range(NNB):
            index = jnp.broadcast_to(nbr[slot], (COLS, BLK, slabs, NB)).astype(jnp.int32)
            picked.append(jnp.take_along_axis(ext, index, axis=3))
        stacked = jnp.stack(picked, axis=2).astype(jnp.float32)
        image = jnp.einsum("kabmn,cbkmn->camn", jac, stacked)
        contrib = jnp.einsum("kabmn,camn->mcbkn", jac, weights.astype(jnp.float32))

        def scatter(terms, index):
            start = jnp.zeros((COLS, BLK, width), jnp.float32)
            return start.at[:, :, index.reshape(-1)].add(terms.reshape(COLS, BLK, NNB * NB))

        spread = jax.vmap(scatter, in_axes=(0, 1))(contrib[:, :, :, 1:], nbr)
        spread = jnp.moveaxis(spread, 0, 2)
        own = spread[..., :NB] + jnp.moveaxis(contrib[:, :, :, 0], 0, 2)
        return image, own, spread[..., NB:NB + HALO], spread[..., NB + HALO:NB + 2 * HALO]

    image, own, downward, upward = lax.map(one_instance, (jac_all, extended, adjoint_view))
    downward = lax.optimization_barrier(downward.astype(jnp.bfloat16)).astype(jnp.float32)
    upward = lax.optimization_barrier(upward.astype(jnp.bfloat16)).astype(jnp.float32)
    down_flat = downward.reshape(lead, slabs, HALO)
    up_flat = upward.reshape(lead, slabs, HALO)
    nothing = jnp.zeros((lead, 1, HALO), jnp.float32)
    from_above = jnp.concatenate([down_flat[:, 1:], nothing], axis=1)
    from_below = jnp.concatenate([nothing, up_flat[:, :-1]], axis=1)
    own = own.reshape(lead, slabs, NB)
    own = add_slab(own, high_idx, from_above)
    own = add_slab(own, low_idx, from_below)
    ids = jnp.arange(inst_count, dtype=jnp.int32)
    table = spectral_table(ids, ids, inst_count, frequency)
    tangent_spec = jnp.einsum("ij,jcbr->icbr", table, tangent_rows.astype(jnp.float32), precision=lax.Precision.HIGHEST)
    adjoint_spec = jnp.einsum("ji,jcbr->icbr", table, adjoint_rows.astype(jnp.float32), precision=lax.Precision.HIGHEST)
    tangent_out = (image.reshape(inst_count, COLS, BLK, ROWS) + tangent_spec).astype(jnp.bfloat16)
    adjoint_out = (own.reshape(inst_count, COLS, BLK, ROWS) + adjoint_spec).astype(jnp.bfloat16)
    return (from_rows(tangent_out), from_rows(adjoint_out))
```

```python
import math

import jax
import jax.numpy as jnp
from jax import lax
from jax.experimental import pallas as pl
from jax.experimental.pallas import tpu as pltpu
from jax.sharding import PartitionSpec as P

INST = 8
VMEM = pl.BlockSpec(memory_space=pltpu.VMEM)
SMEM = pl.BlockSpec(memory_space=pltpu.SMEM)
ANY = pl.BlockSpec(memory_space=pl.ANY)
HBM = pl.BlockSpec(memory_space=pltpu.HBM)


def coefficient(distance):
    parity = 1.0 - 2.0 * (distance % 2)
    return 0.5 * parity * math.cos(math.pi * distance / INST) / math.sin(math.pi * distance / INST)


def side_and_odd():
    sides = lax.axis_size("inst") // INST
    return lax.axis_index("inst") % sides, lax.axis_index("mesh") % 2


def picked_side(ref, side):
    return jnp.where(side == 0, ref[0], ref[1])


def send_matrix(low_ref, high_ref, columns, rows):
    side, odd = side_and_odd()
    low = jnp.where(side == 0, low_ref[0:1], low_ref[1:2])
    high = jnp.where(side == 0, high_ref[0:1], high_ref[1:2])
    first = jnp.where(odd == 1, low, high)
    second = jnp.where(odd == 1, high, low)
    places = [part + rows * c for part in (first, second) for c in range(columns)]
    target = jnp.concatenate(places, axis=1)
    at = lax.broadcasted_iota(jnp.int32, (columns * rows, target.shape[1]), 0)
    return (at == target).astype(jnp.float32).astype(jnp.bfloat16)


def neighbor_matrix(near_ref, rows, halo):
    side, odd = side_and_odd()
    near = picked_side(near_ref, side)
    swapped = jnp.where(near >= rows + halo, near - halo, near + halo)
    inside = near < rows
    outside = jnp.where(odd == 1, near, swapped)
    index = jnp.where(inside, near, jnp.where(near >= rows + 2 * halo, -1, outside))
    slots = near.shape[0]
    wide = jnp.concatenate([index[k : k + 1] for k in range(slots)], axis=1)
    at = lax.broadcasted_iota(jnp.int32, (2 * rows, slots * rows), 0)
    return (at == wide).astype(jnp.float32).astype(jnp.bfloat16)


def copied(pairs, sem):
    copies = [pltpu.make_async_copy(source, target, sem.at[i]) for i, (source, target) in enumerate(pairs)]
    for copy in copies:
        copy.start()
    return copies


def wait_all(copies):
    for copy in copies:
        copy.wait()


def pack_kernel(tangent_hbm, adjoint_hbm, chunks_ref, sem):
    wait_all(copied([(tangent_hbm, chunks_ref.at[:, 0]), (adjoint_hbm, chunks_ref.at[:, 1])], sem))


def adjoint_kernel(
    jac_hbm, adjoint_hbm, tangent_hbm, near_hbm, low_hbm, high_hbm, own_ref, first_ref, second_ref,
    jac_ref, sem, adjoint_ref, tangent_ref, near_ref, low_ref, high_ref, small_sem, weights, high, low
):
    small = copied(
        [
            (adjoint_hbm, adjoint_ref),
            (tangent_hbm, tangent_ref),
            (near_hbm, near_ref),
            (low_hbm, low_ref),
            (high_hbm, high_ref),
        ],
        small_sem,
    )
    columns, block, rows = adjoint_ref.shape[1:]
    slots = jac_ref.shape[0]
    halo = rows // columns
    copies = copied([(jac_hbm.at[0, k], jac_ref.at[k]) for k in range(slots)], sem)
    wait_all(small)
    rows_out = send_matrix(low_ref, high_ref, columns, rows)
    wide = jnp.concatenate([tangent_ref[0, c] for c in range(columns)], axis=1)
    out = jnp.dot(wide, rows_out, preferred_element_type=jnp.float32).astype(jnp.bfloat16)
    first_ref[:block] = out[:, :rows]
    second_ref[:block] = out[:, rows:]
    for c in range(columns):
        weights[c] = adjoint_ref[0, c].astype(jnp.float32)

    def one_slot(k, keep):
        def step(a, acc):
            jac = jac_ref[k, a].astype(jnp.float32)
            return tuple(acc[c] + jac * weights[c, pl.ds(a, 1), :] for c in range(columns))

        zero = tuple(jnp.zeros((block, rows), jnp.float32) for _ in range(columns))
        acc = lax.fori_loop(0, block, step, zero, unroll=8)
        for c in range(columns):
            keep(c, acc[c])

    def keep_own(c, value):
        own_ref[c] = value

    copies[0].wait()
    one_slot(0, keep_own)

    def other_slot(k, carry):
        def keep(c, value):
            top = value.astype(jnp.bfloat16)
            at = pl.ds(pl.multiple_of((k - 1) * rows, rows), rows)
            high[c, :, at] = top
            low[c, :, at] = (value - top.astype(jnp.float32)).astype(jnp.bfloat16)

        pltpu.make_async_copy(jac_hbm.at[0, k], jac_ref.at[k], sem.at[k]).wait()
        one_slot(k, keep)
        return carry

    lax.fori_loop(1, slots, other_slot, 0)
    matrix = neighbor_matrix(near_ref, rows, halo)
    transposed = (((1,), (1,)), ((), ()))
    lane = lax.broadcasted_iota(jnp.int32, (block, rows), 1)
    first = jnp.zeros((block, rows), jnp.float32)
    second = jnp.zeros((block, rows), jnp.float32)
    for c in range(columns):
        q = lax.dot_general(high[c], matrix, transposed, preferred_element_type=jnp.float32)
        q = q + lax.dot_general(low[c], matrix, transposed, preferred_element_type=jnp.float32)
        own_ref[c] = own_ref[c] + q[:, :rows]
        edge = q[:, rows:]
        here = lane // halo == c
        first = jnp.where(here, pltpu.roll(edge, (halo * c) % rows, 1), first)
        second = jnp.where(here, pltpu.roll(edge, (halo * c - halo) % rows, 1), second)
    first_ref[block:] = first.astype(jnp.bfloat16)
    second_ref[block:] = second.astype(jnp.bfloat16)


def tangent_kernel(
    jac_hbm, tangent_hbm, near_hbm, low_hbm, high_hbm, first_ref, second_ref, own_ref, mixed_ref, image_ref, sum_ref,
    jac_ref, sem, tangent_ref, near_ref, low_ref, high_ref, small_sem, picked, partial
):
    small = copied(
        [(tangent_hbm, tangent_ref), (near_hbm, near_ref), (low_hbm, low_ref), (high_hbm, high_ref)], small_sem
    )
    columns, block, rows = tangent_ref.shape[1:]
    slots = jac_ref.shape[0]
    halo = rows // columns
    group = 4
    deep = 16
    loads = sem.shape[0]
    load = block // loads
    parts = [pl.ds(part * load, load) for part in range(loads)]
    copies = copied([(jac_hbm.at[0, :, at], jac_ref.at[:, at]) for at in parts], sem)
    wait_all(small)
    matrix = neighbor_matrix(near_ref, rows, halo)
    lane = lax.broadcasted_iota(jnp.int32, (block, rows), 1)
    first = first_ref[:block].astype(jnp.float32)
    second = second_ref[:block].astype(jnp.float32)
    for c in range(columns):
        edge = jnp.where(
            lane < halo,
            pltpu.roll(first, (rows - halo * c) % rows, 1),
            pltpu.roll(second, (rows + halo - halo * c) % rows, 1),
        ).astype(jnp.bfloat16)
        own = tangent_ref[0, c]
        wide = jnp.dot(jnp.concatenate([own, edge], axis=1), matrix, preferred_element_type=jnp.float32)
        picked[c, :block] = own.astype(jnp.float32)
        for k in range(slots - 1):
            picked[c, (k + 1) * block : (k + 2) * block] = wide[:, k * rows : (k + 1) * rows]

    def one_group(g, carry):
        acc = [[jnp.zeros((8, rows), jnp.float32) for _ in range(columns)] for _ in range(group)]
        for k in range(slots):
            for b in range(0, block, deep):
                x = [picked[c, k * block + b : k * block + b + deep] for c in range(columns)]
                for a in range(group):
                    jac = jac_ref[k, g * group + a, b : b + deep, :].astype(jnp.float32)
                    for c in range(columns):
                        product = jac * x[c]
                        acc[a][c] = acc[a][c] + product[:8] + product[8:]
        for a in range(group):
            for c in range(columns):
                at = pl.multiple_of((c * block + g * group + a) * 8, 8)
                partial[pl.ds(at, 8), :] = acc[a][c]
        return carry

    per = load // group
    for part in range(loads):
        copies[part].wait()
        lax.fori_loop(part * per, (part + 1) * per, one_group, 0)
    for c in range(columns):
        for a in range(0, block, 8):
            base = (c * block + a) * 8
            total = partial[pl.ds(base, 8, stride=8), :]
            for s in range(1, 8):
                total = total + partial[pl.ds(base + s, 8, stride=8), :]
            image_ref[c, a : a + 8] = total
    back = jnp.concatenate([first_ref[block:], second_ref[block:]], axis=1)
    out = send_matrix(low_ref, high_ref, columns, rows)
    added = lax.dot_general(back, out, (((1,), (1,)), ((), ())), preferred_element_type=jnp.float32)
    for c in range(columns):
        sum_ref[c] = own_ref[c] + added[:, c * rows : (c + 1) * rows]


def mix_kernel(frequency_ref, chunks_ref, after_ref, mixed_ref):
    count = chunks_ref.shape[0]
    frequency = frequency_ref[0]
    for panel, sign in ((0, 1.0), (1, -1.0)):
        x = [chunks_ref[j, panel].astype(jnp.float32) for j in range(count)]
        for i in range(count):
            total = None
            for j in range(count):
                if i != j:
                    term = (coefficient((i - j) % count) * sign) * x[j]
                    total = term if total is None else total + term
            mixed_ref[i, panel] = (total * frequency).astype(jnp.bfloat16)


def last_kernel(image_ref, sum_ref, mixed_ref, tangent_ref, adjoint_ref):
    for out_ref, part_ref, panel in ((tangent_ref, image_ref, 0), (adjoint_ref, sum_ref, 1)):
        out_ref[...] = (part_ref[...] + mixed_ref[:, panel].astype(jnp.float32)).astype(jnp.bfloat16)


def call(kernel, out, inputs, specs, scratch=(), flops=0, bytes_accessed=0):
    return pl.pallas_call(
        kernel,
        out_shape=out,
        in_specs=specs,
        out_specs=jax.tree.map(lambda _: VMEM, out),
        scratch_shapes=list(scratch),
        cost_estimate=pl.CostEstimate(flops=flops, bytes_accessed=bytes_accessed, transcendentals=0),
        compiler_params=pltpu.CompilerParams(vmem_limit_bytes=40 << 20),
    )(*inputs)


def body(tangent_in, adjoint_in, jacobian, neighbors, send_low, send_high, frequency):
    _, columns, block, rows = tangent_in.shape
    slots = jacobian.shape[1]
    sides = lax.axis_size("inst") // INST
    mesh_size = lax.axis_size("mesh")
    slabs = sides * mesh_size
    groups = [[side + sides * i for i in range(INST)] for side in range(sides)]

    def device(instance, slab):
        return (instance * sides + slab // mesh_size) * mesh_size + slab % mesh_size

    def pairs(start):
        found = []
        for instance in range(INST):
            for slab in range(start, slabs - 1, 2):
                low, high = device(instance, slab), device(instance, slab + 1)
                found += [(low, high), (high, low)]
        return found

    def exchanged(first, second):
        second = lax.ppermute(second, ("inst", "mesh"), pairs(1))
        first = lax.ppermute(first, ("inst", "mesh"), pairs(0))
        return first, second

    def swapped(chunks):
        return lax.all_to_all(chunks, "inst", 0, 0, axis_index_groups=groups, tiled=True)

    f32, b16 = jnp.float32, jnp.bfloat16
    shape = jax.ShapeDtypeStruct
    chunk = shape((INST, 2, columns * block // INST, rows), b16)
    edge = shape((2 * block, rows), b16)
    panel = shape((columns, block, rows), f32)
    loaded = pltpu.VMEM((slots, block, block, rows), b16)
    dma = pltpu.SemaphoreType.DMA
    copy_of = lambda array: pltpu.VMEM(array.shape, array.dtype)
    split = lambda array: array.reshape((INST, columns * block // INST, rows))
    chunks = call(pack_kernel, chunk, (split(tangent_in), split(adjoint_in)), [HBM] * 2, [dma((2,))], bytes_accessed=1 << 19)
    chunks = swapped(chunks)
    small = (adjoint_in, tangent_in, neighbors, send_low, send_high)
    own, first, second = call(
        adjoint_kernel,
        (panel, edge, edge),
        (jacobian, *small),
        [HBM] * 6,
        [
            loaded,
            dma((slots,)),
            *map(copy_of, small),
            dma((len(small),)),
            pltpu.VMEM((columns, block, rows), f32),
            pltpu.VMEM((columns, block, (slots - 1) * rows), b16),
            pltpu.VMEM((columns, block, (slots - 1) * rows), b16),
        ],
        flops=1 << 32,
        bytes_accessed=6 << 20,
    )
    first, second = exchanged(first, second)
    mixed = call(mix_kernel, chunk, (frequency, chunks, own), [SMEM, VMEM, ANY], bytes_accessed=1 << 19)
    back = swapped(mixed)
    small = small[1:]
    image, total = call(
        tangent_kernel,
        (panel, panel),
        (jacobian, *small, first, second, own, mixed),
        [HBM] * 5 + [VMEM] * 3 + [ANY],
        [
            loaded,
            dma((4,)),
            *map(copy_of, small),
            dma((len(small),)),
            pltpu.VMEM((columns, slots * block, rows), f32),
            pltpu.VMEM((columns * block * 8, rows), f32),
        ],
        flops=1 << 32,
        bytes_accessed=6 << 20,
    )
    out = shape((INST, columns * block // INST, rows), b16)
    tangent_out, adjoint_out = call(last_kernel, (out, out), (split(image), split(total), back), [VMEM] * 3, bytes_accessed=1 << 19)
    return tangent_out.reshape(tangent_in.shape), adjoint_out.reshape(tangent_in.shape)


def solution(mesh):
    in_specs = (
        P("inst", None, None, "mesh"),
        P("inst", None, None, "mesh"),
        P("inst", None, None, None, "mesh"),
        P(None, None, "mesh"),
        P(None, "mesh"),
        P(None, "mesh"),
        P(),
    )
    out_specs = (P("inst", None, None, "mesh"), P("inst", None, None, "mesh"))
    return jax.shard_map(body, mesh=mesh, in_specs=in_specs, out_specs=out_specs, check_vma=False)
```

```python
import math

import jax
import jax.numpy as jnp
from jax import lax
from jax.experimental import pallas as pl
from jax.experimental.pallas import tpu as pltpu
from jax.sharding import PartitionSpec as P

INST = 8
HALF = INST // 2
VMEM = pl.BlockSpec(memory_space=pltpu.VMEM)
SMEM = pl.BlockSpec(memory_space=pltpu.SMEM)
ANY = pl.BlockSpec(memory_space=pl.ANY)


def coefficient(distance):
    parity = 1.0 - 2.0 * (distance % 2)
    return 0.5 * parity * math.cos(math.pi * distance / INST) / math.sin(math.pi * distance / INST)


def place():
    instance = lax.axis_index("inst") // (lax.axis_size("inst") // INST)
    return instance // HALF, instance % HALF


def side_and_odd():
    sides = lax.axis_size("inst") // INST
    return lax.axis_index("inst") % sides, lax.axis_index("mesh") % 2


def picked_side(ref, side):
    return jnp.where(side == 0, ref[0], ref[1])


def send_matrix(low_ref, high_ref, columns, rows):
    side, odd = side_and_odd()
    low = jnp.where(side == 0, low_ref[0:1], low_ref[1:2])
    high = jnp.where(side == 0, high_ref[0:1], high_ref[1:2])
    first = jnp.where(odd == 1, low, high)
    second = jnp.where(odd == 1, high, low)
    places = [part + rows * c for part in (first, second) for c in range(columns)]
    target = jnp.concatenate(places, axis=1)
    at = lax.broadcasted_iota(jnp.int32, (columns * rows, target.shape[1]), 0)
    return (at == target).astype(jnp.float32).astype(jnp.bfloat16)


def neighbor_matrix(near_ref, rows, halo):
    side, odd = side_and_odd()
    near = picked_side(near_ref, side)
    swapped = jnp.where(near >= rows + halo, near - halo, near + halo)
    inside = near < rows
    outside = jnp.where(odd == 1, near, swapped)
    index = jnp.where(inside, near, jnp.where(near >= rows + 2 * halo, -1, outside))
    slots = near.shape[0]
    wide = jnp.concatenate([index[k : k + 1] for k in range(slots)], axis=1)
    at = lax.broadcasted_iota(jnp.int32, (2 * rows, slots * rows), 0)
    return (at == wide).astype(jnp.float32).astype(jnp.bfloat16)


def copied(pairs, sem):
    copies = [pltpu.make_async_copy(source, target, sem.at[i]) for i, (source, target) in enumerate(pairs)]
    for copy in copies:
        copy.start()
    return copies


def half_kernel(half_ref):
    half_ref[...] = jnp.full(half_ref.shape, place()[0], jnp.int32)


def pair_kernel(tangent_ref, adjoint_ref, partner_ref, after_ref, pair_ref, difference_ref):
    upper = place()[0] == 1
    mine = jnp.where(upper, adjoint_ref[0], tangent_ref[0])
    other = partner_ref[0]
    first, second = jnp.where(upper, other, mine), jnp.where(upper, mine, other)
    pair_ref[0], pair_ref[1] = first, second
    difference_ref[...] = (first.astype(jnp.float32) - second.astype(jnp.float32)).astype(jnp.bfloat16)


def adjoint_kernel(
    jac_hbm, adjoint_ref, tangent_ref, near_ref, low_ref, high_ref, own_ref, first_ref, second_ref,
    jac_ref, sem, weights, high, low
):
    columns, block, rows = adjoint_ref.shape[1:]
    slots = jac_ref.shape[0]
    halo = rows // columns
    copies = copied([(jac_hbm.at[0, k], jac_ref.at[k]) for k in range(slots)], sem)
    rows_out = send_matrix(low_ref, high_ref, columns, rows)
    wide = jnp.concatenate([tangent_ref[0, c] for c in range(columns)], axis=1)
    out = jnp.dot(wide, rows_out, preferred_element_type=jnp.float32).astype(jnp.bfloat16)
    first_ref[:block] = out[:, :rows]
    second_ref[:block] = out[:, rows:]
    for c in range(columns):
        weights[c] = adjoint_ref[0, c].astype(jnp.float32)

    def one_slot(k, keep):
        def step(a, acc):
            jac = jac_ref[k, a].astype(jnp.float32)
            return tuple(acc[c] + jac * weights[c, pl.ds(a, 1), :] for c in range(columns))

        zero = tuple(jnp.zeros((block, rows), jnp.float32) for _ in range(columns))
        acc = lax.fori_loop(0, block, step, zero, unroll=8)
        for c in range(columns):
            keep(c, acc[c])

    def keep_own(c, value):
        own_ref[c] = value

    copies[0].wait()
    one_slot(0, keep_own)

    def other_slot(k, carry):
        def keep(c, value):
            top = value.astype(jnp.bfloat16)
            at = pl.ds(pl.multiple_of((k - 1) * rows, rows), rows)
            high[c, :, at] = top
            low[c, :, at] = (value - top.astype(jnp.float32)).astype(jnp.bfloat16)

        pltpu.make_async_copy(jac_hbm.at[0, k], jac_ref.at[k], sem.at[k]).wait()
        one_slot(k, keep)
        return carry

    lax.fori_loop(1, slots, other_slot, 0)
    matrix = neighbor_matrix(near_ref, rows, halo)
    transposed = (((1,), (1,)), ((), ()))
    lane = lax.broadcasted_iota(jnp.int32, (block, rows), 1)
    first = jnp.zeros((block, rows), jnp.float32)
    second = jnp.zeros((block, rows), jnp.float32)
    for c in range(columns):
        q = lax.dot_general(high[c], matrix, transposed, preferred_element_type=jnp.float32)
        q = q + lax.dot_general(low[c], matrix, transposed, preferred_element_type=jnp.float32)
        own_ref[c] = own_ref[c] + q[:, :rows]
        edge = q[:, rows:]
        here = lane // halo == c
        first = jnp.where(here, pltpu.roll(edge, (halo * c) % rows, 1), first)
        second = jnp.where(here, pltpu.roll(edge, (halo * c - halo) % rows, 1), second)
    first_ref[block:] = first.astype(jnp.bfloat16)
    second_ref[block:] = second.astype(jnp.bfloat16)


def tangent_kernel(
    jac_hbm, tangent_ref, near_ref, low_ref, high_ref, first_ref, second_ref, own_ref, mixed_ref, image_ref, sum_ref,
    jac_ref, sem, picked, partial
):
    columns, block, rows = tangent_ref.shape[1:]
    slots = jac_ref.shape[0]
    halo = rows // columns
    group = 4
    deep = 16
    loads = sem.shape[0]
    load = block // loads
    parts = [pl.ds(part * load, load) for part in range(loads)]
    copies = copied([(jac_hbm.at[0, :, at], jac_ref.at[:, at]) for at in parts], sem)
    matrix = neighbor_matrix(near_ref, rows, halo)
    lane = lax.broadcasted_iota(jnp.int32, (block, rows), 1)
    first = first_ref[:block].astype(jnp.float32)
    second = second_ref[:block].astype(jnp.float32)
    for c in range(columns):
        edge = jnp.where(
            lane < halo,
            pltpu.roll(first, (rows - halo * c) % rows, 1),
            pltpu.roll(second, (rows + halo - halo * c) % rows, 1),
        ).astype(jnp.bfloat16)
        own = tangent_ref[0, c]
        wide = jnp.dot(jnp.concatenate([own, edge], axis=1), matrix, preferred_element_type=jnp.float32)
        picked[c, :block] = own.astype(jnp.float32)
        for k in range(slots - 1):
            picked[c, (k + 1) * block : (k + 2) * block] = wide[:, k * rows : (k + 1) * rows]

    def one_group(g, carry):
        acc = [[jnp.zeros((8, rows), jnp.float32) for _ in range(columns)] for _ in range(group)]
        for k in range(slots):
            for b in range(0, block, deep):
                x = [picked[c, k * block + b : k * block + b + deep] for c in range(columns)]
                for a in range(group):
                    jac = jac_ref[k, g * group + a, b : b + deep, :].astype(jnp.float32)
                    for c in range(columns):
                        product = jac * x[c]
                        acc[a][c] = acc[a][c] + product[:8] + product[8:]
        for a in range(group):
            for c in range(columns):
                at = pl.multiple_of((c * block + g * group + a) * 8, 8)
                partial[pl.ds(at, 8), :] = acc[a][c]
        return carry

    per = load // group
    for part in range(loads):
        copies[part].wait()
        lax.fori_loop(part * per, (part + 1) * per, one_group, 0)
    for c in range(columns):
        for a in range(0, block, 8):
            base = (c * block + a) * 8
            total = partial[pl.ds(base, 8, stride=8), :]
            for s in range(1, 8):
                total = total + partial[pl.ds(base + s, 8, stride=8), :]
            image_ref[c, a : a + 8] = total
    back = jnp.concatenate([first_ref[block:], second_ref[block:]], axis=1)
    out = send_matrix(low_ref, high_ref, columns, rows)
    added = lax.dot_general(back, out, (((1,), (1,)), ((), ())), preferred_element_type=jnp.float32)
    for c in range(columns):
        sum_ref[c] = own_ref[c] + added[:, c * rows : (c + 1) * rows]


def mix_kernel(frequency_ref, pair_ref, behind_ref, ahead_ref, across_ref, after_ref, keep_ref, send_ref):
    half, at = place()
    upper = half == 1
    scale = jnp.where(upper, -frequency_ref[0], frequency_ref[0])

    def factors(distance, wrapped):
        same, other = coefficient(distance % INST), coefficient((distance + HALF) % INST)
        return jnp.where(wrapped, other, same) * scale, jnp.where(wrapped, same, other) * scale

    across, across_other = factors(-2, at >= 2)
    terms = [
        (behind_ref, factors(1, at == 0)),
        (ahead_ref, factors(-1, at == HALF - 1)),
    ]
    own = coefficient(HALF) * scale
    for c in range(pair_ref.shape[1]):
        first, second = pair_ref[0, c].astype(jnp.float32), pair_ref[1, c].astype(jnp.float32)
        difference = across_ref[c].astype(jnp.float32)
        a = own * second + across * difference
        b = own * first + across_other * difference
        for ref, (same, other) in terms:
            first, second = ref[0, c].astype(jnp.float32), ref[1, c].astype(jnp.float32)
            a = a + same * first + other * second
            b = b + other * first + same * second
        keep_ref[c] = jnp.where(upper, b, a)
        send_ref[c] = jnp.where(upper, a, b).astype(jnp.bfloat16)


def last_kernel(image_ref, sum_ref, keep_ref, partner_ref, tangent_ref, adjoint_ref):
    upper = place()[0] == 1
    for c in range(image_ref.shape[0]):
        keep, other = keep_ref[c], partner_ref[c].astype(jnp.float32)
        tangent_ref[0, c] = (image_ref[c] + jnp.where(upper, other, keep)).astype(jnp.bfloat16)
        adjoint_ref[0, c] = (sum_ref[c] + jnp.where(upper, keep, other)).astype(jnp.bfloat16)


def call(kernel, out, inputs, specs, scratch=(), flops=0, bytes_accessed=0):
    return pl.pallas_call(
        kernel,
        out_shape=out,
        in_specs=specs,
        out_specs=jax.tree.map(lambda _: VMEM, out),
        scratch_shapes=list(scratch),
        cost_estimate=pl.CostEstimate(flops=flops, bytes_accessed=bytes_accessed, transcendentals=0),
        compiler_params=pltpu.CompilerParams(vmem_limit_bytes=52 << 20),
    )(*inputs)


def body(tangent_in, adjoint_in, jacobian, neighbors, send_low, send_high, frequency):
    _, columns, block, rows = tangent_in.shape
    slots = jacobian.shape[1]
    sides = lax.axis_size("inst") // INST
    mesh_size = lax.axis_size("mesh")
    slabs = sides * mesh_size

    def device(instance, slab):
        return (instance * sides + slab // mesh_size) * mesh_size + slab % mesh_size

    def pairs(start):
        found = []
        for instance in range(INST):
            for slab in range(start, slabs - 1, 2):
                low, high = device(instance, slab), device(instance, slab + 1)
                found += [(low, high), (high, low)]
        return found

    def exchanged(first, second):
        second = lax.ppermute(second, ("inst", "mesh"), pairs(1))
        first = lax.ppermute(first, ("inst", "mesh"), pairs(0))
        return first, second

    def moved(value, target):
        return lax.ppermute(value, "inst", [(i * sides + side, target(i) * sides + side) for i in range(INST) for side in range(sides)])

    def partner(i):
        return (i + HALF) % INST

    def along(step):
        return lambda i: i // HALF * HALF + (i + step) % HALF

    f32, b16 = jnp.float32, jnp.bfloat16
    shape = jax.ShapeDtypeStruct
    edge = shape((2 * block, rows), b16)
    panel = shape((columns, block, rows), f32)
    loaded = pltpu.VMEM((slots, block, block, rows), b16)
    dma = pltpu.SemaphoreType.DMA
    half = call(half_kernel, shape((8, 128), jnp.int32), (), [], flops=1 << 34)
    partner_in = moved(jnp.where(half[0, 0] == 0, adjoint_in, tangent_in), partner)
    small = (adjoint_in, tangent_in, neighbors, send_low, send_high)
    own, first, second = call(
        adjoint_kernel,
        (panel, edge, edge),
        (jacobian, *small),
        [ANY] + [VMEM] * 5,
        [
            loaded,
            dma((slots,)),
            pltpu.VMEM((columns, block, rows), f32),
            pltpu.VMEM((columns, block, (slots - 1) * rows), b16),
            pltpu.VMEM((columns, block, (slots - 1) * rows), b16),
        ],
        flops=1 << 32,
        bytes_accessed=6 << 20,
    )
    panels = shape((2, columns, block, rows), b16)
    one = shape((columns, block, rows), b16)
    pair, difference = call(
        pair_kernel, (panels, one), (tangent_in, adjoint_in, partner_in, own), [VMEM] * 3 + [ANY], bytes_accessed=1 << 19
    )
    across = moved(difference, along(2))
    behind = moved(pair, along(1))
    ahead = moved(pair, along(-1))
    first, second = exchanged(first, second)
    small = small[1:]
    image, total = call(
        tangent_kernel,
        (panel, panel),
        (jacobian, *small, first, second, own, pair),
        [ANY] + [VMEM] * 7 + [ANY],
        [
            loaded,
            dma((4,)),
            pltpu.VMEM((columns, slots * block, rows), f32),
            pltpu.VMEM((columns * block * 8, rows), f32),
        ],
        flops=1 << 32,
        bytes_accessed=6 << 20,
    )
    keep, send = call(
        mix_kernel,
        (panel, one),
        (frequency, pair, behind, ahead, across, image),
        [SMEM] + [VMEM] * 4 + [ANY],
        bytes_accessed=1 << 19,
    )
    other = moved(send, partner)
    out = shape(tangent_in.shape, b16)
    return call(last_kernel, (out, out), (image, total, keep, other), [VMEM] * 4, bytes_accessed=1 << 19)


def solution(mesh):
    in_specs = (
        P("inst", None, None, "mesh"),
        P("inst", None, None, "mesh"),
        P("inst", None, None, None, "mesh"),
        P(None, None, "mesh"),
        P(None, "mesh"),
        P(None, "mesh"),
        P(),
    )
    out_specs = (P("inst", None, None, "mesh"), P("inst", None, None, "mesh"))
    return jax.shard_map(body, mesh=mesh, in_specs=in_specs, out_specs=out_specs, check_vma=False)
```

```python
import math

import jax
import jax.numpy as jnp
from jax import lax
from jax.experimental import pallas as pl
from jax.experimental.pallas import tpu as pltpu
from jax.sharding import PartitionSpec as P

INST = 8
HALF = INST // 2
VMEM = pl.BlockSpec(memory_space=pltpu.VMEM)
ANY = pl.BlockSpec(memory_space=pl.ANY)


def coefficient(distance):
    parity = 1.0 - 2.0 * (distance % 2)
    return 0.5 * parity * math.cos(math.pi * distance / INST) / math.sin(math.pi * distance / INST)


def place():
    instance = lax.axis_index("inst") // (lax.axis_size("inst") // INST)
    return instance // HALF, instance % HALF


def side_and_odd():
    sides = lax.axis_size("inst") // INST
    return lax.axis_index("inst") % sides, lax.axis_index("mesh") % 2


def picked_side(ref, side):
    return jnp.where(side == 0, ref[0], ref[1])


def send_matrix(low_ref, high_ref, columns, rows):
    side, odd = side_and_odd()
    low = jnp.where(side == 0, low_ref[0:1], low_ref[1:2])
    high = jnp.where(side == 0, high_ref[0:1], high_ref[1:2])
    first = jnp.where(odd == 1, low, high)
    second = jnp.where(odd == 1, high, low)
    places = [part + rows * c for part in (first, second) for c in range(columns)]
    target = jnp.concatenate(places, axis=1)
    at = lax.broadcasted_iota(jnp.int32, (columns * rows, target.shape[1]), 0)
    return (at == target).astype(jnp.float32).astype(jnp.bfloat16)


def neighbor_matrix(near_ref, rows, halo):
    side, odd = side_and_odd()
    near = picked_side(near_ref, side)
    swapped = jnp.where(near >= rows + halo, near - halo, near + halo)
    inside = near < rows
    outside = jnp.where(odd == 1, near, swapped)
    index = jnp.where(inside, near, jnp.where(near >= rows + 2 * halo, -1, outside))
    slots = near.shape[0]
    wide = jnp.concatenate([index[k : k + 1] for k in range(slots)], axis=1)
    at = lax.broadcasted_iota(jnp.int32, (2 * rows, slots * rows), 0)
    return (at == wide).astype(jnp.float32).astype(jnp.bfloat16)


def half_kernel(half_ref):
    half_ref[...] = jnp.full(half_ref.shape, place()[0], jnp.int32)


def pair_kernel(tangent_ref, adjoint_ref, partner_ref, after_ref, pair_ref, difference_ref):
    upper = place()[0] == 1
    mine = jnp.where(upper, adjoint_ref[0], tangent_ref[0])
    other = partner_ref[0]
    first, second = jnp.where(upper, other, mine), jnp.where(upper, mine, other)
    pair_ref[0], pair_ref[1] = first, second
    difference_ref[...] = (first.astype(jnp.float32) - second.astype(jnp.float32)).astype(jnp.bfloat16)


def slot_products(jac_ref, weights, slot):
    columns, block, rows = weights.shape

    def step(a, acc):
        jac = jac_ref[0, slot, a].astype(jnp.float32)
        return tuple(acc[c] + jac * weights[c, pl.ds(a, 1), :] for c in range(columns))

    zero = tuple(jnp.zeros((block, rows), jnp.float32) for _ in range(columns))
    return lax.fori_loop(0, block, step, zero, unroll=16)


def neighbor_products(jac_ref, adjoint_ref, high, low, weights, start, stop):
    columns, _, rows = weights.shape
    for c in range(columns):
        weights[c] = adjoint_ref[0, c].astype(jnp.float32)

    def one_slot(k, carry):
        acc = slot_products(jac_ref, weights, k)
        at = pl.ds(pl.multiple_of((k - start) * rows, rows), rows)
        for c in range(columns):
            top = acc[c].astype(jnp.bfloat16)
            high[c, :, at] = top
            low[c, :, at] = (acc[c] - top.astype(jnp.float32)).astype(jnp.bfloat16)
        return carry

    lax.fori_loop(start, stop, one_slot, 0)


def adjoint_kernel(jac_ref, adjoint_ref, high_ref, low_ref, weights):
    count = high_ref.shape[2] // weights.shape[2]
    neighbor_products(jac_ref, adjoint_ref, high_ref, low_ref, weights, 1, 1 + count)


def return_kernel(
    jac_ref, adjoint_ref, tangent_ref, near_ref, send_low_ref, send_high_ref, high_ref, low_ref, after_ref, after_too_ref,
    own_ref, first_ref, second_ref, weights, high, low
):
    columns, block, rows = weights.shape
    halo = rows // columns
    done = high_ref.shape[2] // rows
    rows_out = send_matrix(send_low_ref, send_high_ref, columns, rows)
    wide = jnp.concatenate([tangent_ref[0, c] for c in range(columns)], axis=1)
    out = jnp.dot(wide, rows_out, preferred_element_type=jnp.float32).astype(jnp.bfloat16)
    first_ref[:block] = out[:, :rows]
    second_ref[:block] = out[:, rows:]
    neighbor_products(jac_ref, adjoint_ref, high, low, weights, 1 + done, jac_ref.shape[1])
    own = slot_products(jac_ref, weights, 0)
    matrix = neighbor_matrix(near_ref, rows, halo)
    before, after = matrix[:, : done * rows], matrix[:, done * rows :]
    transposed = (((1,), (1,)), ((), ()))
    lane = lax.broadcasted_iota(jnp.int32, (block, rows), 1)
    first = jnp.zeros((block, rows), jnp.float32)
    second = jnp.zeros((block, rows), jnp.float32)
    for c in range(columns):
        q = sum(
            lax.dot_general(ref[c], part, transposed, preferred_element_type=jnp.float32)
            for ref, part in ((high_ref, before), (low_ref, before), (high, after), (low, after))
        )
        own_ref[c] = own[c] + q[:, :rows]
        edge = q[:, rows:]
        here = lane // halo == c
        first = jnp.where(here, pltpu.roll(edge, (halo * c) % rows, 1), first)
        second = jnp.where(here, pltpu.roll(edge, (halo * c - halo) % rows, 1), second)
    first_ref[block:] = first.astype(jnp.bfloat16)
    second_ref[block:] = second.astype(jnp.bfloat16)


def tangent_kernel(
    jac_ref, tangent_ref, near_ref, low_ref, high_ref, first_ref, second_ref, own_ref, after_ref, image_ref, sum_ref, picked, partial
):
    columns, block, rows = tangent_ref.shape[1:]
    slots = jac_ref.shape[1]
    halo = rows // columns
    group = 8
    deep = 16
    matrix = neighbor_matrix(near_ref, rows, halo)
    lane = lax.broadcasted_iota(jnp.int32, (block, rows), 1)
    first = first_ref[:block].astype(jnp.float32)
    second = second_ref[:block].astype(jnp.float32)
    for c in range(columns):
        edge = jnp.where(
            lane < halo,
            pltpu.roll(first, (rows - halo * c) % rows, 1),
            pltpu.roll(second, (rows + halo - halo * c) % rows, 1),
        ).astype(jnp.bfloat16)
        own = tangent_ref[0, c]
        wide = jnp.dot(jnp.concatenate([own, edge], axis=1), matrix, preferred_element_type=jnp.float32)
        picked[c, :block] = own.astype(jnp.float32)
        for k in range(slots - 1):
            picked[c, (k + 1) * block : (k + 2) * block] = wide[:, k * rows : (k + 1) * rows]

    back = jnp.concatenate([first_ref[block:], second_ref[block:]], axis=1)
    out = send_matrix(low_ref, high_ref, columns, rows)
    added = lax.dot_general(back, out, (((1,), (1,)), ((), ())), preferred_element_type=jnp.float32)
    for c in range(columns):
        sum_ref[c] = own_ref[c] + added[:, c * rows : (c + 1) * rows]

    def one_group(g, carry):
        acc = [[jnp.zeros((8, rows), jnp.float32) for _ in range(columns)] for _ in range(group)]
        for k in range(slots):
            for b in range(0, block, deep):
                x = [picked[c, k * block + b : k * block + b + deep] for c in range(columns)]
                for a in range(group):
                    jac = jac_ref[0, k, g * group + a, b : b + deep, :].astype(jnp.float32)
                    for c in range(columns):
                        product = jac * x[c]
                        acc[a][c] = acc[a][c] + (product[:8] + product[8:])
        for c in range(columns):
            for a in range(group):
                partial[c, a * 8 : (a + 1) * 8] = acc[a][c]
        at = pl.ds(pl.multiple_of(g * group, group), group)
        for c in range(columns):
            total = partial[c, pl.ds(0, 8, stride=8), :]
            for s in range(1, 8):
                total = total + partial[c, pl.ds(s, 8, stride=8), :]
            image_ref[c, at] = total
        return carry

    lax.fori_loop(0, block // group, one_group, 0)


def mix_kernel(frequency_ref, pair_ref, behind_ref, ahead_ref, across_ref, after_ref, keep_ref, send_ref):
    half, at = place()
    upper = half == 1
    frequency = frequency_ref[...]
    scale = jnp.where(upper, -frequency, frequency)

    def factors(distance, wrapped):
        same, other = coefficient(distance % INST), coefficient((distance + HALF) % INST)
        return jnp.where(wrapped, other, same) * scale, jnp.where(wrapped, same, other) * scale

    across, across_other = factors(-2, at >= 2)
    terms = [
        (behind_ref, factors(1, at == 0)),
        (ahead_ref, factors(-1, at == HALF - 1)),
    ]
    own = coefficient(HALF) * scale
    for c in range(pair_ref.shape[1]):
        first, second = pair_ref[0, c].astype(jnp.float32), pair_ref[1, c].astype(jnp.float32)
        difference = across_ref[c].astype(jnp.float32)
        a = own * second + across * difference
        b = own * first + across_other * difference
        for ref, (same, other) in terms:
            first, second = ref[0, c].astype(jnp.float32), ref[1, c].astype(jnp.float32)
            a = a + same * first + other * second
            b = b + other * first + same * second
        keep_ref[c] = jnp.where(upper, b, a)
        send_ref[c] = jnp.where(upper, a, b).astype(jnp.bfloat16)


def last_kernel(image_ref, sum_ref, keep_ref, partner_ref, tangent_ref, adjoint_ref):
    upper = place()[0] == 1
    for c in range(image_ref.shape[0]):
        keep, other = keep_ref[c], partner_ref[c].astype(jnp.float32)
        tangent_ref[0, c] = (image_ref[c] + jnp.where(upper, other, keep)).astype(jnp.bfloat16)
        adjoint_ref[0, c] = (sum_ref[c] + jnp.where(upper, keep, other)).astype(jnp.bfloat16)


def call(kernel, out, inputs, specs, scratch=(), flops=0, bytes_accessed=0):
    return pl.pallas_call(
        kernel,
        out_shape=out,
        in_specs=specs,
        out_specs=jax.tree.map(lambda _: VMEM, out),
        scratch_shapes=list(scratch),
        cost_estimate=pl.CostEstimate(flops=flops, bytes_accessed=bytes_accessed, transcendentals=0),
        compiler_params=pltpu.CompilerParams(vmem_limit_bytes=44 << 20),
    )(*inputs)


def body(tangent_in, adjoint_in, jacobian, neighbors, send_low, send_high, frequency):
    _, columns, block, rows = tangent_in.shape
    slots = jacobian.shape[1]
    sides = lax.axis_size("inst") // INST
    mesh_size = lax.axis_size("mesh")
    slabs = sides * mesh_size

    def device(instance, slab):
        return (instance * sides + slab // mesh_size) * mesh_size + slab % mesh_size

    def pairs(start):
        found = []
        for instance in range(INST):
            for slab in range(start, slabs - 1, 2):
                low, high = device(instance, slab), device(instance, slab + 1)
                found += [(low, high), (high, low)]
        return found

    def exchanged(first, second):
        second = lax.ppermute(second, ("inst", "mesh"), pairs(1))
        first = lax.ppermute(first, ("inst", "mesh"), pairs(0))
        return first, second

    def moved(value, target):
        return lax.ppermute(value, "inst", [(i * sides + side, target(i) * sides + side) for i in range(INST) for side in range(sides)])

    def partner(i):
        return (i + HALF) % INST

    def along(step):
        return lambda i: i // HALF * HALF + (i + step) % HALF

    f32, b16 = jnp.float32, jnp.bfloat16
    shape = jax.ShapeDtypeStruct
    edge = shape((2 * block, rows), b16)
    panel = shape((columns, block, rows), f32)
    half = call(half_kernel, shape((1, rows), jnp.int32), (), [], flops=1 << 34)
    partner_in = moved(jnp.where(half.reshape((1, 1, 1, rows)) == 0, adjoint_in, tangent_in), partner)
    weights = pltpu.VMEM((columns, block, rows), f32)
    done = (slots + 1) // 2
    later = slots - 1 - done
    high, low = call(
        adjoint_kernel,
        (shape((columns, block, done * rows), b16),) * 2,
        (jacobian, adjoint_in),
        [VMEM] * 2,
        [weights],
        flops=1 << 31,
        bytes_accessed=6 << 20,
    )
    panels = shape((2, columns, block, rows), b16)
    one = shape((columns, block, rows), b16)
    pair, difference = call(
        pair_kernel, (panels, one), (tangent_in, adjoint_in, partner_in, high), [VMEM] * 3 + [ANY], bytes_accessed=1 << 19
    )
    across = moved(difference, along(2))
    behind = moved(pair, along(1))
    ahead = moved(pair, along(-1))
    own, first, second = call(
        return_kernel,
        (panel, edge, edge),
        (jacobian, adjoint_in, tangent_in, neighbors, send_low, send_high, high, low, pair, difference),
        [VMEM] * 8 + [ANY] * 2,
        [weights] + [pltpu.VMEM((columns, block, later * rows), b16)] * 2,
        flops=1 << 31,
        bytes_accessed=6 << 20,
    )
    first, second = exchanged(first, second)
    keep, send = call(
        mix_kernel,
        (panel, one),
        (frequency.reshape((1, 1)), pair, behind, ahead, across, own),
        [VMEM] * 5 + [ANY],
        bytes_accessed=1 << 19,
    )
    other = moved(send, partner)
    image, total = call(
        tangent_kernel,
        (panel, panel),
        (jacobian, tangent_in, neighbors, send_low, send_high, first, second, own, keep),
        [VMEM] * 8 + [ANY],
        [pltpu.VMEM((columns, slots * block, rows), f32), pltpu.VMEM((columns, 64, rows), f32)],
        flops=1 << 32,
        bytes_accessed=6 << 20,
    )
    out = shape(tangent_in.shape, b16)
    return call(last_kernel, (out, out), (image, total, keep, other), [VMEM] * 4, bytes_accessed=1 << 19)


def solution(mesh):
    in_specs = (
        P("inst", None, None, "mesh"),
        P("inst", None, None, "mesh"),
        P("inst", None, None, None, "mesh"),
        P(None, None, "mesh"),
        P(None, "mesh"),
        P(None, "mesh"),
        P(),
    )
    out_specs = (P("inst", None, None, "mesh"), P("inst", None, None, "mesh"))
    return jax.shard_map(body, mesh=mesh, in_specs=in_specs, out_specs=out_specs, check_vma=False)
```

```python
import math

import jax
import jax.numpy as jnp
from jax import lax
from jax.experimental import pallas as pl
from jax.experimental.pallas import tpu as pltpu
from jax.sharding import PartitionSpec as P

INST = 8
HALF = INST // 2
VMEM = pl.BlockSpec(memory_space=pltpu.VMEM)
ANY = pl.BlockSpec(memory_space=pl.ANY)


def coefficient(distance):
    parity = 1.0 - 2.0 * (distance % 2)
    return 0.5 * parity * math.cos(math.pi * distance / INST) / math.sin(math.pi * distance / INST)


def place():
    instance = lax.axis_index("inst") // (lax.axis_size("inst") // INST)
    return instance // HALF, instance % HALF


def side_and_odd():
    sides = lax.axis_size("inst") // INST
    return lax.axis_index("inst") % sides, lax.axis_index("mesh") % 2


def at_end():
    side, _ = side_and_odd()
    slab = side * lax.axis_size("mesh") + lax.axis_index("mesh")
    return (slab == 0) | (slab == lax.axis_size("inst") // INST * lax.axis_size("mesh") - 1)


def picked_side(ref, side):
    return jnp.where(side == 0, ref[0], ref[1])


def send_matrix(low_ref, high_ref, columns, rows):
    side, odd = side_and_odd()
    low = jnp.where(side == 0, low_ref[0:1], low_ref[1:2])
    high = jnp.where(side == 0, high_ref[0:1], high_ref[1:2])
    first = jnp.where(odd == 1, low, high)
    second = jnp.where(odd == 1, high, low)
    second = jnp.where(at_end(), -columns * rows, second)
    places = [part + rows * c for part in (first, second) for c in range(columns)]
    target = jnp.concatenate(places, axis=1)
    at = lax.broadcasted_iota(jnp.int32, (columns * rows, target.shape[1]), 0)
    return (at == target).astype(jnp.float32).astype(jnp.bfloat16)


def neighbor_matrix(near_ref, rows, halo):
    side, odd = side_and_odd()
    near = picked_side(near_ref, side)
    swapped = jnp.where(near >= rows + halo, near - halo, near + halo)
    inside = near < rows
    outside = jnp.where(odd == 1, near, swapped)
    outside = jnp.where(at_end() & (outside >= rows + halo), -1, outside)
    index = jnp.where(inside, near, jnp.where(near >= rows + 2 * halo, -1, outside))
    slots = near.shape[0]
    wide = jnp.concatenate([index[k : k + 1] for k in range(slots)], axis=1)
    at = lax.broadcasted_iota(jnp.int32, (2 * rows, slots * rows), 0)
    return (at == wide).astype(jnp.float32).astype(jnp.bfloat16)


def half_kernel(half_ref):
    half_ref[...] = jnp.full(half_ref.shape, place()[0], jnp.int32)


def pair_kernel(tangent_ref, adjoint_ref, partner_ref, after_ref, pair_ref, difference_ref):
    upper = place()[0] == 1
    mine = jnp.where(upper, adjoint_ref[0], tangent_ref[0])
    other = partner_ref[0]
    first, second = jnp.where(upper, other, mine), jnp.where(upper, mine, other)
    pair_ref[0], pair_ref[1] = first, second
    difference_ref[...] = (first.astype(jnp.float32) - second.astype(jnp.float32)).astype(jnp.bfloat16)


def slot_products(jac_ref, weights, slot):
    columns, block, rows = weights.shape

    def step(a, acc):
        jac = jac_ref[0, slot, a].astype(jnp.float32)
        return tuple(acc[c] + jac * weights[c, pl.ds(a, 1), :] for c in range(columns))

    zero = tuple(jnp.zeros((block, rows), jnp.float32) for _ in range(columns))
    return lax.fori_loop(0, block, step, zero, unroll=16)


def neighbor_products(jac_ref, adjoint_ref, high, low, weights, start, stop):
    columns, _, rows = weights.shape
    for c in range(columns):
        weights[c] = adjoint_ref[0, c].astype(jnp.float32)

    def one_slot(k, carry):
        acc = slot_products(jac_ref, weights, k)
        at = pl.ds(pl.multiple_of((k - start) * rows, rows), rows)
        for c in range(columns):
            top = acc[c].astype(jnp.bfloat16)
            high[c, :, at] = top
            low[c, :, at] = (acc[c] - top.astype(jnp.float32)).astype(jnp.bfloat16)
        return carry

    lax.fori_loop(start, stop, one_slot, 0)


def adjoint_kernel(jac_ref, adjoint_ref, frequency_hbm, high_ref, low_ref, frequency_ref, weights, scalar, sem):
    copy = pltpu.make_async_copy(frequency_hbm, scalar, sem)
    copy.start()
    count = high_ref.shape[2] // weights.shape[2]
    neighbor_products(jac_ref, adjoint_ref, high_ref, low_ref, weights, 1, 1 + count)
    copy.wait()
    frequency_ref[...] = jnp.full(frequency_ref.shape, scalar[0])


def return_kernel(
    jac_ref, adjoint_ref, tangent_ref, near_ref, send_low_ref, send_high_ref, high_ref, low_ref, after_ref, after_too_ref,
    own_ref, first_ref, second_ref, weights, high, low
):
    columns, block, rows = weights.shape
    halo = rows // columns
    done = high_ref.shape[2] // rows
    rows_out = send_matrix(send_low_ref, send_high_ref, columns, rows)
    wide = jnp.concatenate([tangent_ref[0, c] for c in range(columns)], axis=1)
    out = jnp.dot(wide, rows_out, preferred_element_type=jnp.float32).astype(jnp.bfloat16)
    first_ref[:block] = out[:, :rows]
    second_ref[:block] = out[:, rows:]
    neighbor_products(jac_ref, adjoint_ref, high, low, weights, 1 + done, jac_ref.shape[1])
    own = slot_products(jac_ref, weights, 0)
    matrix = neighbor_matrix(near_ref, rows, halo)
    before, after = matrix[:, : done * rows], matrix[:, done * rows :]
    transposed = (((1,), (1,)), ((), ()))
    lane = lax.broadcasted_iota(jnp.int32, (block, rows), 1)
    first = jnp.zeros((block, rows), jnp.float32)
    second = jnp.zeros((block, rows), jnp.float32)
    for c in range(columns):
        q = sum(
            lax.dot_general(ref[c], part, transposed, preferred_element_type=jnp.float32)
            for ref, part in ((high_ref, before), (low_ref, before), (high, after), (low, after))
        )
        own_ref[c] = own[c] + q[:, :rows]
        edge = q[:, rows:]
        here = lane // halo == c
        first = jnp.where(here, pltpu.roll(edge, (halo * c) % rows, 1), first)
        second = jnp.where(here, pltpu.roll(edge, (halo * c - halo) % rows, 1), second)
    first_ref[block:] = first.astype(jnp.bfloat16)
    second_ref[block:] = second.astype(jnp.bfloat16)


def tangent_kernel(
    jac_ref, tangent_ref, near_ref, low_ref, high_ref, first_ref, second_ref, own_ref, after_ref, image_ref, sum_ref, picked, partial
):
    columns, block, rows = tangent_ref.shape[1:]
    slots = jac_ref.shape[1]
    halo = rows // columns
    group = 8
    deep = 16
    matrix = neighbor_matrix(near_ref, rows, halo)
    lane = lax.broadcasted_iota(jnp.int32, (block, rows), 1)
    first = first_ref[:block].astype(jnp.float32)
    second = second_ref[:block].astype(jnp.float32)
    for c in range(columns):
        edge = jnp.where(
            lane < halo,
            pltpu.roll(first, (rows - halo * c) % rows, 1),
            pltpu.roll(second, (rows + halo - halo * c) % rows, 1),
        ).astype(jnp.bfloat16)
        own = tangent_ref[0, c]
        wide = jnp.dot(jnp.concatenate([own, edge], axis=1), matrix, preferred_element_type=jnp.float32)
        picked[c, :block] = own.astype(jnp.float32)
        for k in range(slots - 1):
            picked[c, (k + 1) * block : (k + 2) * block] = wide[:, k * rows : (k + 1) * rows]

    back = jnp.concatenate([first_ref[block:], second_ref[block:]], axis=1)
    out = send_matrix(low_ref, high_ref, columns, rows)
    added = lax.dot_general(back, out, (((1,), (1,)), ((), ())), preferred_element_type=jnp.float32)
    for c in range(columns):
        sum_ref[c] = own_ref[c] + added[:, c * rows : (c + 1) * rows]

    def one_group(g, carry):
        acc = [[jnp.zeros((8, rows), jnp.float32) for _ in range(columns)] for _ in range(group)]
        for k in range(slots):
            for b in range(0, block, deep):
                x = [picked[c, k * block + b : k * block + b + deep] for c in range(columns)]
                for a in range(group):
                    jac = jac_ref[0, k, g * group + a, b : b + deep, :].astype(jnp.float32)
                    for c in range(columns):
                        product = jac * x[c]
                        acc[a][c] = acc[a][c] + (product[:8] + product[8:])
        for c in range(columns):
            for a in range(group):
                partial[c, a * 8 : (a + 1) * 8] = acc[a][c]
        at = pl.ds(pl.multiple_of(g * group, group), group)
        for c in range(columns):
            total = partial[c, pl.ds(0, 8, stride=8), :]
            for s in range(1, 8):
                total = total + partial[c, pl.ds(s, 8, stride=8), :]
            image_ref[c, at] = total
        return carry

    lax.fori_loop(0, block // group, one_group, 0)


def mix_kernel(frequency_ref, pair_ref, behind_ref, ahead_ref, across_ref, after_ref, keep_ref, send_ref):
    half, at = place()
    upper = half == 1
    frequency = frequency_ref[...]
    scale = jnp.where(upper, -frequency, frequency)

    def factors(distance, wrapped):
        same, other = coefficient(distance % INST), coefficient((distance + HALF) % INST)
        return jnp.where(wrapped, other, same) * scale, jnp.where(wrapped, same, other) * scale

    across, across_other = factors(-2, at >= 2)
    terms = [
        (behind_ref, factors(1, at == 0)),
        (ahead_ref, factors(-1, at == HALF - 1)),
    ]
    own = coefficient(HALF) * scale
    for c in range(pair_ref.shape[1]):
        first, second = pair_ref[0, c].astype(jnp.float32), pair_ref[1, c].astype(jnp.float32)
        difference = across_ref[c].astype(jnp.float32)
        a = own * second + across * difference
        b = own * first + across_other * difference
        for ref, (same, other) in terms:
            first, second = ref[0, c].astype(jnp.float32), ref[1, c].astype(jnp.float32)
            a = a + same * first + other * second
            b = b + other * first + same * second
        keep_ref[c] = jnp.where(upper, b, a)
        send_ref[c] = jnp.where(upper, a, b).astype(jnp.bfloat16)


def last_kernel(image_ref, sum_ref, keep_ref, partner_ref, tangent_ref, adjoint_ref):
    upper = place()[0] == 1
    for c in range(image_ref.shape[0]):
        keep, other = keep_ref[c], partner_ref[c].astype(jnp.float32)
        tangent_ref[0, c] = (image_ref[c] + jnp.where(upper, other, keep)).astype(jnp.bfloat16)
        adjoint_ref[0, c] = (sum_ref[c] + jnp.where(upper, keep, other)).astype(jnp.bfloat16)


def call(kernel, out, inputs, specs, scratch=(), flops=0, bytes_accessed=0):
    return pl.pallas_call(
        kernel,
        out_shape=out,
        in_specs=specs,
        out_specs=jax.tree.map(lambda _: VMEM, out),
        scratch_shapes=list(scratch),
        cost_estimate=pl.CostEstimate(flops=flops, bytes_accessed=bytes_accessed, transcendentals=0),
        compiler_params=pltpu.CompilerParams(vmem_limit_bytes=44 << 20),
    )(*inputs)


def body(tangent_in, adjoint_in, jacobian, neighbors, send_low, send_high, frequency):
    _, columns, block, rows = tangent_in.shape
    slots = jacobian.shape[1]
    sides = lax.axis_size("inst") // INST
    mesh_size = lax.axis_size("mesh")
    slabs = sides * mesh_size

    def device(instance, slab):
        return (instance * sides + slab // mesh_size) * mesh_size + slab % mesh_size

    def pairs(start):
        found = []
        for instance in range(INST):
            for slab in range(start, slabs - 1, 2):
                low, high = device(instance, slab), device(instance, slab + 1)
                found += [(low, high), (high, low)]
            if start == 1:
                low, high = device(instance, 0), device(instance, slabs - 1)
                found += [(low, high), (high, low)]
        return found

    def exchanged(first, second):
        second = lax.ppermute(second, ("inst", "mesh"), pairs(1))
        first = lax.ppermute(first, ("inst", "mesh"), pairs(0))
        return first, second

    def moved(value, target):
        return lax.ppermute(value, "inst", [(i * sides + side, target(i) * sides + side) for i in range(INST) for side in range(sides)])

    def partner(i):
        return (i + HALF) % INST

    def along(step):
        return lambda i: i // HALF * HALF + (i + step) % HALF

    f32, b16 = jnp.float32, jnp.bfloat16
    shape = jax.ShapeDtypeStruct
    edge = shape((2 * block, rows), b16)
    panel = shape((columns, block, rows), f32)
    half = call(half_kernel, shape((1, rows), jnp.int32), (), [], flops=1 << 34)
    partner_in = moved(jnp.where(half.reshape((1, 1, 1, rows)) == 0, adjoint_in, tangent_in), partner)
    weights = pltpu.VMEM((columns, block, rows), f32)
    done = (slots + 1) // 2
    later = slots - 1 - done
    half_terms = shape((columns, block, done * rows), b16)
    high, low, frequency = call(
        adjoint_kernel,
        (half_terms, half_terms, shape((1, rows), f32)),
        (jacobian, adjoint_in, frequency),
        [VMEM] * 2 + [ANY],
        [weights, pltpu.SMEM((1,), f32), pltpu.SemaphoreType.DMA],
        flops=1 << 31,
        bytes_accessed=6 << 20,
    )
    panels = shape((2, columns, block, rows), b16)
    one = shape((columns, block, rows), b16)
    pair, difference = call(
        pair_kernel, (panels, one), (tangent_in, adjoint_in, partner_in, high), [VMEM] * 3 + [ANY], bytes_accessed=1 << 19
    )
    across = moved(difference, along(2))
    behind = moved(pair, along(1))
    ahead = moved(pair, along(-1))
    own, first, second = call(
        return_kernel,
        (panel, edge, edge),
        (jacobian, adjoint_in, tangent_in, neighbors, send_low, send_high, high, low, pair, difference),
        [VMEM] * 8 + [ANY] * 2,
        [weights] + [pltpu.VMEM((columns, block, later * rows), b16)] * 2,
        flops=1 << 31,
        bytes_accessed=6 << 20,
    )
    first, second = exchanged(first, second)
    keep, send = call(
        mix_kernel,
        (panel, one),
        (frequency, pair, behind, ahead, across, own),
        [VMEM] * 5 + [ANY],
        bytes_accessed=1 << 19,
    )
    other = moved(send, partner)
    image, total = call(
        tangent_kernel,
        (panel, panel),
        (jacobian, tangent_in, neighbors, send_low, send_high, first, second, own, keep),
        [VMEM] * 8 + [ANY],
        [pltpu.VMEM((columns, slots * block, rows), f32), pltpu.VMEM((columns, 64, rows), f32)],
        flops=1 << 32,
        bytes_accessed=6 << 20,
    )
    out = shape(tangent_in.shape, b16)
    return call(last_kernel, (out, out), (image, total, keep, other), [VMEM] * 4, bytes_accessed=1 << 19)


def solution(mesh):
    in_specs = (
        P("inst", None, None, "mesh"),
        P("inst", None, None, "mesh"),
        P("inst", None, None, None, "mesh"),
        P(None, None, "mesh"),
        P(None, "mesh"),
        P(None, "mesh"),
        P(),
    )
    out_specs = (P("inst", None, None, "mesh"), P("inst", None, None, "mesh"))
    return jax.shard_map(body, mesh=mesh, in_specs=in_specs, out_specs=out_specs, check_vma=False)
```

```python
import math

import jax
import jax.numpy as jnp
from jax import lax
from jax.experimental import pallas as pl
from jax.experimental.pallas import tpu as pltpu
from jax.sharding import PartitionSpec as P

INST = 8
HALF = INST // 2
VMEM = pl.BlockSpec(memory_space=pltpu.VMEM)
ANY = pl.BlockSpec(memory_space=pl.ANY)


def coefficient(distance):
    parity = 1.0 - 2.0 * (distance % 2)
    return 0.5 * parity * math.cos(math.pi * distance / INST) / math.sin(math.pi * distance / INST)


def place():
    instance = lax.axis_index("inst") // (lax.axis_size("inst") // INST)
    return instance // HALF, instance % HALF


def side_and_odd():
    sides = lax.axis_size("inst") // INST
    return lax.axis_index("inst") % sides, lax.axis_index("mesh") % 2


def at_end():
    side, _ = side_and_odd()
    slab = side * lax.axis_size("mesh") + lax.axis_index("mesh")
    return (slab == 0) | (slab == lax.axis_size("inst") // INST * lax.axis_size("mesh") - 1)


def picked_side(ref, side):
    return jnp.where(side == 0, ref[0], ref[1])


def send_matrix(low_ref, high_ref, columns, rows):
    side, odd = side_and_odd()
    low = jnp.where(side == 0, low_ref[0:1], low_ref[1:2])
    high = jnp.where(side == 0, high_ref[0:1], high_ref[1:2])
    first = jnp.where(odd == 1, low, high)
    second = jnp.where(odd == 1, high, low)
    second = jnp.where(at_end(), -columns * rows, second)
    places = [part + rows * c for part in (first, second) for c in range(columns)]
    target = jnp.concatenate(places, axis=1)
    at = lax.broadcasted_iota(jnp.int32, (columns * rows, target.shape[1]), 0)
    return (at == target).astype(jnp.float32).astype(jnp.bfloat16)


def neighbor_matrix(near_ref, rows, halo):
    side, odd = side_and_odd()
    near = picked_side(near_ref, side)
    swapped = jnp.where(near >= rows + halo, near - halo, near + halo)
    inside = near < rows
    outside = jnp.where(odd == 1, near, swapped)
    outside = jnp.where(at_end() & (outside >= rows + halo), -1, outside)
    index = jnp.where(inside, near, jnp.where(near >= rows + 2 * halo, -1, outside))
    slots = near.shape[0]
    wide = jnp.concatenate([index[k : k + 1] for k in range(slots)], axis=1)
    at = lax.broadcasted_iota(jnp.int32, (2 * rows, slots * rows), 0)
    return (at == wide).astype(jnp.float32).astype(jnp.bfloat16)


def half_kernel(half_ref):
    half_ref[...] = jnp.full(half_ref.shape, place()[0], jnp.int32)


def pair_kernel(tangent_ref, adjoint_ref, partner_ref, after_ref, pair_ref, difference_ref):
    upper = place()[0] == 1
    mine = jnp.where(upper, adjoint_ref[0], tangent_ref[0])
    other = partner_ref[0]
    first, second = jnp.where(upper, other, mine), jnp.where(upper, mine, other)
    pair_ref[0], pair_ref[1] = first, second
    difference_ref[...] = (first.astype(jnp.float32) - second.astype(jnp.float32)).astype(jnp.bfloat16)


def slot_products(jac_ref, weights, slot):
    columns, block, rows = weights.shape

    def step(a, acc):
        jac = jac_ref[0, slot, a].astype(jnp.float32)
        return tuple(acc[c] + jac * weights[c, pl.ds(a, 1), :] for c in range(columns))

    zero = tuple(jnp.zeros((block, rows), jnp.float32) for _ in range(columns))
    return lax.fori_loop(0, block, step, zero, unroll=16)


def neighbor_products(jac_ref, adjoint_ref, high, low, weights, start, stop):
    columns, _, rows = weights.shape
    for c in range(columns):
        weights[c] = adjoint_ref[0, c].astype(jnp.float32)

    def one_slot(k, carry):
        acc = slot_products(jac_ref, weights, k)
        at = pl.ds(pl.multiple_of((k - start) * rows, rows), rows)
        for c in range(columns):
            top = acc[c].astype(jnp.bfloat16)
            high[c, :, at] = top
            low[c, :, at] = (acc[c] - top.astype(jnp.float32)).astype(jnp.bfloat16)
        return carry

    lax.fori_loop(start, stop, one_slot, 0)


def adjoint_kernel(
    jac_ref, adjoint_ref, near_ref, send_low_ref, send_high_ref, frequency_hbm, high_ref, low_ref, near_matrix_ref, send_matrix_ref,
    frequency_ref, weights, scalar, sem
):
    copy = pltpu.make_async_copy(frequency_hbm, scalar, sem)
    copy.start()
    count = high_ref.shape[2] // weights.shape[2]
    neighbor_products(jac_ref, adjoint_ref, high_ref, low_ref, weights, 1, 1 + count)
    columns, _, rows = weights.shape
    near_matrix_ref[...] = neighbor_matrix(near_ref, rows, rows // columns)
    send_matrix_ref[...] = send_matrix(send_low_ref, send_high_ref, columns, rows)
    copy.wait()
    frequency_ref[...] = jnp.full(frequency_ref.shape, scalar[0])


def return_kernel(
    jac_ref, adjoint_ref, tangent_ref, near_matrix_ref, send_matrix_ref, high_ref, low_ref, after_ref, after_too_ref,
    own_ref, first_ref, second_ref, weights, high, low
):
    columns, block, rows = weights.shape
    halo = rows // columns
    done = high_ref.shape[2] // rows
    rows_out = send_matrix_ref[...]
    wide = jnp.concatenate([tangent_ref[0, c] for c in range(columns)], axis=1)
    out = jnp.dot(wide, rows_out, preferred_element_type=jnp.float32).astype(jnp.bfloat16)
    first_ref[:block] = out[:, :rows]
    second_ref[:block] = out[:, rows:]
    neighbor_products(jac_ref, adjoint_ref, high, low, weights, 1 + done, jac_ref.shape[1])
    own = slot_products(jac_ref, weights, 0)
    before, after = near_matrix_ref[:, : done * rows], near_matrix_ref[:, done * rows :]
    transposed = (((1,), (1,)), ((), ()))
    lane = lax.broadcasted_iota(jnp.int32, (block, rows), 1)
    first = jnp.zeros((block, rows), jnp.float32)
    second = jnp.zeros((block, rows), jnp.float32)
    for c in range(columns):
        q = sum(
            lax.dot_general(ref[c], part, transposed, preferred_element_type=jnp.float32)
            for ref, part in ((high_ref, before), (low_ref, before), (high, after), (low, after))
        )
        own_ref[c] = own[c] + q[:, :rows]
        edge = q[:, rows:]
        here = lane // halo == c
        first = jnp.where(here, pltpu.roll(edge, (halo * c) % rows, 1), first)
        second = jnp.where(here, pltpu.roll(edge, (halo * c - halo) % rows, 1), second)
    first_ref[block:] = first.astype(jnp.bfloat16)
    second_ref[block:] = second.astype(jnp.bfloat16)


def tangent_kernel(
    jac_ref, tangent_ref, near_matrix_ref, send_matrix_ref, first_ref, second_ref, own_ref, after_ref, image_ref, sum_ref, picked, partial
):
    columns, block, rows = tangent_ref.shape[1:]
    slots = jac_ref.shape[1]
    halo = rows // columns
    group = 8
    deep = 16
    matrix = near_matrix_ref[...]
    lane = lax.broadcasted_iota(jnp.int32, (block, rows), 1)
    first = first_ref[:block].astype(jnp.float32)
    second = second_ref[:block].astype(jnp.float32)
    for c in range(columns):
        edge = jnp.where(
            lane < halo,
            pltpu.roll(first, (rows - halo * c) % rows, 1),
            pltpu.roll(second, (rows + halo - halo * c) % rows, 1),
        ).astype(jnp.bfloat16)
        own = tangent_ref[0, c]
        wide = jnp.dot(jnp.concatenate([own, edge], axis=1), matrix, preferred_element_type=jnp.float32)
        picked[c, :block] = own.astype(jnp.float32)
        for k in range(slots - 1):
            picked[c, (k + 1) * block : (k + 2) * block] = wide[:, k * rows : (k + 1) * rows]

    back = jnp.concatenate([first_ref[block:], second_ref[block:]], axis=1)
    out = send_matrix_ref[...]
    added = lax.dot_general(back, out, (((1,), (1,)), ((), ())), preferred_element_type=jnp.float32)
    for c in range(columns):
        sum_ref[c] = own_ref[c] + added[:, c * rows : (c + 1) * rows]

    def one_group(g, carry):
        acc = [[jnp.zeros((8, rows), jnp.float32) for _ in range(columns)] for _ in range(group)]
        for k in range(slots):
            for b in range(0, block, deep):
                x = [picked[c, k * block + b : k * block + b + deep] for c in range(columns)]
                for a in range(group):
                    jac = jac_ref[0, k, g * group + a, b : b + deep, :].astype(jnp.float32)
                    for c in range(columns):
                        product = jac * x[c]
                        acc[a][c] = acc[a][c] + (product[:8] + product[8:])
        for c in range(columns):
            for a in range(group):
                partial[c, a * 8 : (a + 1) * 8] = acc[a][c]
        at = pl.ds(pl.multiple_of(g * group, group), group)
        for c in range(columns):
            total = partial[c, pl.ds(0, 8, stride=8), :]
            for s in range(1, 8):
                total = total + partial[c, pl.ds(s, 8, stride=8), :]
            image_ref[c, at] = total
        return carry

    lax.fori_loop(0, block // group, one_group, 0)


def mix_kernel(frequency_ref, pair_ref, behind_ref, ahead_ref, across_ref, after_ref, keep_ref, send_ref):
    half, at = place()
    upper = half == 1
    frequency = frequency_ref[...]
    scale = jnp.where(upper, -frequency, frequency)

    def factors(distance, wrapped):
        same, other = coefficient(distance % INST), coefficient((distance + HALF) % INST)
        return jnp.where(wrapped, other, same) * scale, jnp.where(wrapped, same, other) * scale

    across, across_other = factors(-2, at >= 2)
    terms = [
        (behind_ref, factors(1, at == 0)),
        (ahead_ref, factors(-1, at == HALF - 1)),
    ]
    own = coefficient(HALF) * scale
    for c in range(pair_ref.shape[1]):
        first, second = pair_ref[0, c].astype(jnp.float32), pair_ref[1, c].astype(jnp.float32)
        difference = across_ref[c].astype(jnp.float32)
        a = own * second + across * difference
        b = own * first + across_other * difference
        for ref, (same, other) in terms:
            first, second = ref[0, c].astype(jnp.float32), ref[1, c].astype(jnp.float32)
            a = a + same * first + other * second
            b = b + other * first + same * second
        keep_ref[c] = jnp.where(upper, b, a)
        send_ref[c] = jnp.where(upper, a, b).astype(jnp.bfloat16)


def last_kernel(image_ref, sum_ref, keep_ref, partner_ref, tangent_ref, adjoint_ref):
    upper = place()[0] == 1
    for c in range(image_ref.shape[0]):
        keep, other = keep_ref[c], partner_ref[c].astype(jnp.float32)
        tangent_ref[0, c] = (image_ref[c] + jnp.where(upper, other, keep)).astype(jnp.bfloat16)
        adjoint_ref[0, c] = (sum_ref[c] + jnp.where(upper, keep, other)).astype(jnp.bfloat16)


def call(kernel, out, inputs, specs, scratch=(), flops=0, bytes_accessed=0):
    return pl.pallas_call(
        kernel,
        out_shape=out,
        in_specs=specs,
        out_specs=jax.tree.map(lambda _: VMEM, out),
        scratch_shapes=list(scratch),
        cost_estimate=pl.CostEstimate(flops=flops, bytes_accessed=bytes_accessed, transcendentals=0),
        compiler_params=pltpu.CompilerParams(vmem_limit_bytes=44 << 20),
    )(*inputs)


def body(tangent_in, adjoint_in, jacobian, neighbors, send_low, send_high, frequency):
    _, columns, block, rows = tangent_in.shape
    slots = jacobian.shape[1]
    sides = lax.axis_size("inst") // INST
    mesh_size = lax.axis_size("mesh")
    slabs = sides * mesh_size

    def device(instance, slab):
        return (instance * sides + slab // mesh_size) * mesh_size + slab % mesh_size

    def pairs(start):
        found = []
        for instance in range(INST):
            for slab in range(start, slabs - 1, 2):
                low, high = device(instance, slab), device(instance, slab + 1)
                found += [(low, high), (high, low)]
            if start == 1:
                found += [(device(instance, slab), device((instance + HALF) % INST, slab)) for slab in (0, slabs - 1)]
        return found

    def exchanged(first, second):
        second = lax.ppermute(second, ("inst", "mesh"), pairs(1))
        first = lax.ppermute(first, ("inst", "mesh"), pairs(0))
        return first, second

    def moved(value, target):
        return lax.ppermute(value, "inst", [(i * sides + side, target(i) * sides + side) for i in range(INST) for side in range(sides)])

    def partner(i):
        return (i + HALF) % INST

    def along(step):
        return lambda i: i // HALF * HALF + (i + step) % HALF

    f32, b16 = jnp.float32, jnp.bfloat16
    shape = jax.ShapeDtypeStruct
    edge = shape((2 * block, rows), b16)
    panel = shape((columns, block, rows), f32)
    half = call(half_kernel, shape((1, rows), jnp.int32), (), [], flops=1 << 34)
    partner_in = moved(jnp.where(half.reshape((1, 1, 1, rows)) == 0, adjoint_in, tangent_in), partner)
    weights = pltpu.VMEM((columns, block, rows), f32)
    done = (slots + 1) // 2
    later = slots - 1 - done
    half_terms = shape((columns, block, done * rows), b16)
    matrices = shape((2 * rows, (slots - 1) * rows), b16), shape((columns * rows, 2 * rows), b16)
    high, low, near_matrix, out_matrix, frequency = call(
        adjoint_kernel,
        (half_terms, half_terms, *matrices, shape((1, rows), f32)),
        (jacobian, adjoint_in, neighbors, send_low, send_high, frequency),
        [VMEM] * 5 + [ANY],
        [weights, pltpu.SMEM((1,), f32), pltpu.SemaphoreType.DMA],
        flops=1 << 31,
        bytes_accessed=6 << 20,
    )
    panels = shape((2, columns, block, rows), b16)
    one = shape((columns, block, rows), b16)
    pair, difference = call(
        pair_kernel, (panels, one), (tangent_in, adjoint_in, partner_in, high), [VMEM] * 3 + [ANY], bytes_accessed=1 << 19
    )
    across = moved(difference, along(2))
    behind = moved(pair, along(1))
    ahead = moved(pair, along(-1))
    own, first, second = call(
        return_kernel,
        (panel, edge, edge),
        (jacobian, adjoint_in, tangent_in, near_matrix, out_matrix, high, low, pair, difference),
        [VMEM] * 7 + [ANY] * 2,
        [weights] + [pltpu.VMEM((columns, block, later * rows), b16)] * 2,
        flops=1 << 31,
        bytes_accessed=6 << 20,
    )
    first, second = exchanged(first, second)
    keep, send = call(
        mix_kernel,
        (panel, one),
        (frequency, pair, behind, ahead, across, own),
        [VMEM] * 5 + [ANY],
        bytes_accessed=1 << 19,
    )
    other = moved(send, partner)
    image, total = call(
        tangent_kernel,
        (panel, panel),
        (jacobian, tangent_in, near_matrix, out_matrix, first, second, own, keep),
        [VMEM] * 7 + [ANY],
        [pltpu.VMEM((columns, slots * block, rows), f32), pltpu.VMEM((columns, 64, rows), f32)],
        flops=1 << 32,
        bytes_accessed=6 << 20,
    )
    out = shape(tangent_in.shape, b16)
    return call(last_kernel, (out, out), (image, total, keep, other), [VMEM] * 4, bytes_accessed=1 << 19)


def solution(mesh):
    in_specs = (
        P("inst", None, None, "mesh"),
        P("inst", None, None, "mesh"),
        P("inst", None, None, None, "mesh"),
        P(None, None, "mesh"),
        P(None, "mesh"),
        P(None, "mesh"),
        P(),
    )
    out_specs = (P("inst", None, None, "mesh"), P("inst", None, None, "mesh"))
    return jax.shard_map(body, mesh=mesh, in_specs=in_specs, out_specs=out_specs, check_vma=False)
```
